256 devices in a mesh: loop: 64 (over y, z_lo, x, core), occ: 4 (over z_hi).
Axes of the slice: x: 4, y: 4, z: 8 (z_hi: 4, z_lo: 2; z = z_hi * 2 + z_lo), core: 2. Of those that a mesh axis runs over, the one named last changes fastest.
Arguments:
- integrals: bfloat16 [131072, 8192], P('loop', 'occ'), may hold values from -0.0625 to 0.0625
- amplitudes: bfloat16 [512, 8192], P('loop', 'occ'), may hold values from -6 to 6
- tile_list: int32 [512, 2], P('loop'), may hold values from -1 to 49, as said below
- occ_pairs: int32 [512, 2], replicated, may hold values from 0 to 199
- e_occ: float32 [200], replicated, may hold values from -1.5 to -0.3
- e_virt: float32 [800], replicated, may hold values from 0.2 to 2
Outputs:
- increment: float32 [512, 131072], P('occ', 'loop')
The draws below stay inside these ranges and needn't reach their ends.
Inputs may be any that keep to these rules, and one draw needn't show every extreme that they name: tile_list[q] and tile_list[q + 256] are (A, B) and (B, A) with A != B, or both (-1, -1). Live tiles are distinct and lie in one pair-symmetry sector of the orbital tiles' irreps; the first 8 slots are live; at most three quarters of the slots are live.
All inputs are finite; a program needn't handle non-finite values.
Results may differ from the reference program's by a relative error of at most 0.014.
Values may be sent and summed in bfloat16 or wider, within the bound.
A program may use at most 64 MiB of HBM per device.

```python
import jax
import jax.numpy as jnp
from jax import lax

NV = 800
NO = 200
TILE = 16
TILES_DEV = 8
ROWS_DEV = 2048
NT = 512
NR = 131072
CD_DEV = 2048
CD = 8192
PAIRS = 512
N_LOOP = 64
N_OCC = 4


def draw_tile_list(key, part):
    key = jax.random.fold_in(key, 7)
    key_irrep, key_sector, key_order, key_place = jax.random.split(key, 4)
    count = NV // TILE
    filler = jax.random.randint(key_irrep, (count - 8,), 0, 8)
    irreps = jnp.sort(jnp.concatenate([jnp.arange(8, dtype=jnp.int32), filler.astype(jnp.int32)]))
    sector = jax.random.randint(key_sector, (), 1, 8).astype(jnp.int32)
    ids = jnp.arange(count, dtype=jnp.int32)
    lower = ids[:, None] < ids[None, :]
    matching = jnp.bitwise_xor(irreps[:, None], irreps[None, :]) == sector
    allowed = (lower & matching).reshape(-1)
    touches_last = ((ids[:, None] == count - 1) | (ids[None, :] == count - 1)).reshape(-1)
    square = count * count
    ranking = jax.random.permutation(key_order, square).astype(jnp.int32)
    scores = ranking + jnp.where(allowed, 4 * square, 0) + jnp.where(touches_last, 2 * square, 0)
    half = NT // 2
    chosen = lax.top_k(scores, half)[1].astype(jnp.int32)
    ranks = jnp.arange(half, dtype=jnp.int32)
    usable = allowed[chosen] & (ranks < half - half // 4)
    first = jnp.where(usable, chosen // count, -1).astype(jnp.int32)
    second = jnp.where(usable, chosen % count, -1).astype(jnp.int32)
    rest = TILES_DEV + jax.random.permutation(key_place, half - TILES_DEV).astype(jnp.int32)
    places = jnp.concatenate([jnp.arange(TILES_DEV, dtype=jnp.int32), rest])
    top_first = jnp.zeros((half,), jnp.int32).at[places].set(first)
    top_second = jnp.zeros((half,), jnp.int32).at[places].set(second)
    upper = jnp.stack([top_first, top_second], 1)
    bottom = jnp.stack([top_second, top_first], 1)
    return jnp.concatenate([upper, bottom], 0).astype(jnp.int32)


def with_ends(values, own_key, low, high):
    spot = [jax.random.randint(jax.random.fold_in(own_key, axis), (), 0, length) for axis, length in enumerate(values.shape)]
    longest = values.shape.index(max(values.shape))
    neighbour = spot[:longest] + [(spot[longest] + 1) % values.shape[longest]] + spot[longest + 1:]
    return values.at[tuple(spot)].set(low).at[tuple(neighbour)].set(high)


def steps_of(key, dims, pieces, smallest, top_value):
    loudness, own = 1.0, jax.random.fold_in(key, 6)
    for axis_at, blocks in pieces:
        steps = jnp.exp(jax.random.uniform(jax.random.fold_in(own, axis_at), (blocks,), jnp.float32, smallest / len(pieces), top_value / len(pieces)))
        loudness = loudness * jnp.repeat(steps, dims[axis_at] // blocks).reshape([-1 if axis == axis_at else 1 for axis in range(len(dims))])
    return loudness


def centred(key, extent, width, limit, cuts=(), kind=jnp.bfloat16):
    values = width * jax.random.normal(key, extent, jnp.float32)
    if cuts:
        values = values * steps_of(key, extent, cuts, -0.22, 0.18)
    return jnp.clip(values, -limit, limit).astype(kind)


def setup_inputs(seed: int = 0) -> dict:
    keys = jax.random.split(jax.random.key(seed), 7)
    integrals = centred(keys[0], (NR, CD), CD ** -0.5, 0.0625, ((0, 64), (1, 4)))
    amplitudes = centred(keys[1], (PAIRS, CD), 1.0, 6.0, ((0, 64), (1, 4)))
    tile_list = draw_tile_list(jax.random.fold_in(keys[6], 71), 0)
    occ_pairs = with_ends(jax.random.randint(keys[3], (PAIRS, 2), 0, NO), jax.random.fold_in(keys[3], 1), 0, NO - 1).astype(jnp.int32)
    e_occ = jnp.clip(jax.random.uniform(keys[4], (NO,), jnp.float32, -1.5, -0.3), -1.5, -0.3)
    e_virt = jnp.clip(jax.random.uniform(keys[5], (NV,), jnp.float32, 0.2, 2.0), 0.2, 2.0)
    return {"integrals": integrals, "amplitudes": amplitudes, "tile_list": tile_list, "occ_pairs": occ_pairs, "e_occ": e_occ, "e_virt": e_virt}


def ladder_block(block, amplitudes):
    total = jnp.zeros((amplitudes.shape[0], block.shape[0]), jnp.float32)
    for column in range(N_OCC):
        left = amplitudes[:, column * CD_DEV:(column + 1) * CD_DEV]
        right = block[:, column * CD_DEV:(column + 1) * CD_DEV]
        product = lax.dot_general(left, right, (((1,), (1,)), ((), ())), preferred_element_type=jnp.float32)
        rounded = lax.optimization_barrier(product.astype(jnp.bfloat16))
        total = total + rounded.astype(jnp.float32)
    return total


def reference(integrals, amplitudes, tile_list, occ_pairs, e_occ, e_virt):
    stacked = integrals.reshape(N_LOOP, ROWS_DEV, CD)
    blocks = lax.map(lambda block: ladder_block(block, amplitudes), stacked)
    direct = jnp.transpose(blocks, (1, 0, 2)).reshape(PAIRS, NT, TILE, TILE)
    halves = direct.reshape(PAIRS, 2, NT // 2, TILE, TILE)
    mirrored = jnp.swapaxes(halves[:, ::-1], 3, 4).reshape(PAIRS, NT, TILE, TILE)
    summed = direct + mirrored
    offsets = jnp.arange(TILE, dtype=jnp.int32)[None, :]
    first = jnp.maximum(tile_list[:, 0], 0)[:, None] * TILE + offsets
    second = jnp.maximum(tile_list[:, 1], 0)[:, None] * TILE + offsets
    row_energy = e_virt[first][:, :, None] + e_virt[second][:, None, :]
    pair_energy = e_occ[occ_pairs[:, 0]] + e_occ[occ_pairs[:, 1]]
    denom = pair_energy[:, None, None, None] - row_energy[None]
    live = (tile_list[:, 0] >= 0)[None, :, None, None]
    return jnp.where(live, summed / denom, 0.0).reshape(PAIRS, NR)
```

```python
import functools

import jax
import jax.numpy as jnp
from jax import lax
from jax.experimental import pallas as pl
from jax.experimental.pallas import tpu as pltpu
from jax.sharding import PartitionSpec as P

MESH = pl.DeviceIdType.MESH
TILE = 16
WIDTH = TILE * TILE
ROWS = 2048
TILES = ROWS // WIDTH
CD = 2048
HALF = CD // 2
PAIRS = 512
SHARE = 128
NY, NZL, NX, NCORE, NOCC = 4, 2, 4, 2, 4
CHUNK = 128
GROUP = 16
STEP = 512
X_OFF = (0, 1, -1, 2)
BLOCKS = [(dy, dz) for dy in (0, 1, 3, 2) for dz in range(NZL)][1:]
BF16, F32 = jnp.bfloat16, jnp.float32


def kernel(
    ints_hbm, amps_ref, tiles_ref, pairs_ref, e_occ_ref, e_virt_ref, out_hbm,
    ints, own, peer, gath, part, sum1, sum2, low, mirr, outs, inv, pair_e, perm,
    load_sem, store_sem, sib_sem, blk_s, blk_r, fwd_s, fwd_r, x_s, x_r, xf_s, xf_r, z_s, z_r, m_s, m_r,
):
    loop, occ = lax.axis_index("loop"), lax.axis_index("occ")
    core, x, zl, y = loop % 2, (loop // 2) % NX, (loop // 8) % NZL, loop // 16

    def at(dy=0, dz=0, dx=0, dc=0, dh=0):
        yy, zz = (y + dy + NY) % NY, (zl + dz) % NZL
        xx, cc = (x + dx + NX) % NX, (core + dc) % NCORE
        return ((yy * NZL + zz) * NX + xx) * NCORE + cc, (occ + dh + NOCC) % NOCC

    sends = []

    def send(src, dst, send_sem, recv_sem, to):
        copy = pltpu.make_async_remote_copy(
            src_ref=src, dst_ref=dst, send_sem=send_sem, recv_sem=recv_sem,
            device_id=to, device_id_type=MESH,
        )
        copy.start()
        sends.append(copy)
        return copy

    load = pltpu.make_async_copy(ints_hbm, ints, load_sem)
    load.start()

    partners = [at(dc=1), at(dh=1), at(dh=-1)]
    partners += [at(dx=d) for d in X_OFF[1:]]
    partners += [at(dy=dy, dz=dz) for dy, dz in BLOCKS]
    barrier = pltpu.get_barrier_semaphore()
    for partner in partners:
        pl.semaphore_signal(barrier, inc=1, device_id=partner, device_id_type=MESH)
    block = amps_ref[...].astype(F32)
    doubled = jnp.concatenate([block, block], axis=0)
    own[...] = doubled.astype(BF16)
    pl.semaphore_wait(barrier, len(partners))

    swap = send(own, peer, sib_sem.at[0], sib_sem.at[1], at(dc=1))
    swap.wait_recv()
    upper = lax.broadcasted_iota(jnp.int32, (GROUP, CD), 0) < 8
    mine = jnp.logical_xor(upper, core == 1)
    merged = jnp.where(mine, doubled, peer[...].astype(F32)).astype(BF16)

    def block_rows(dy, dz):
        index = ((y + dy + NY) % NY) * NZL + (zl + dz) % NZL
        return pl.ds(pl.multiple_of(index * GROUP, GROUP), GROUP)

    here = block_rows(0, 0)
    gath[0, 0, here, :] = merged[:, :HALF]
    gath[0, 1, here, :] = merged[:, HALF:]

    blocks = []
    for i, (dy, dz) in enumerate(BLOCKS):
        mine_at = gath.at[0, core, here, :]
        blocks.append(send(mine_at, mine_at, blk_s.at[i], blk_r.at[i], at(dy=dy, dz=dz)))

    row_at = lax.broadcasted_iota(jnp.int32, (WIDTH, WIDTH), 0)
    col_at = lax.broadcasted_iota(jnp.int32, (WIDTH, WIDTH), 1)
    hit = col_at == (row_at % TILE) * TILE + row_at // TILE
    perm[...] = jnp.where(hit, 1.0, 0.0).astype(BF16)
    sub = lax.broadcasted_iota(jnp.int32, (8, 128), 0)

    def pair_body(g, carry):
        rows = jnp.zeros((8, 128), F32)
        for i in range(8):
            pair = occ * SHARE + g * 8 + i
            energy = e_occ_ref[pairs_ref[0, pair]] + e_occ_ref[pairs_ref[1, pair]]
            rows = jnp.where(sub == i, energy, rows)
        pair_e[pl.ds(pl.multiple_of(g * 8, 8), 8), :] = rows
        return carry

    lax.fori_loop(0, SHARE // 8, pair_body, 0)
    lane = lax.broadcasted_iota(jnp.int32, (8, WIDTH), 1)
    lane_x, lane_y = lane // TILE, lane % TILE

    def tile_body(t, carry):
        first, second = tiles_ref[0, t], tiles_ref[1, t]
        a, b = jnp.maximum(first, 0) * TILE, jnp.maximum(second, 0) * TILE
        e_a = jnp.zeros((8, WIDTH), F32)
        e_b = jnp.zeros((8, WIDTH), F32)
        for i in range(TILE):
            e_a = jnp.where(lane_x == i, e_virt_ref[a + i], e_a)
            e_b = jnp.where(lane_y == i, e_virt_ref[b + i], e_b)
        energy = e_a + e_b
        keep = jnp.full((8, WIDTH), first, jnp.int32) >= 0
        for g in range(SHARE // 8):
            pair = pair_e[g * 8:(g + 1) * 8, :]
            denom = jnp.concatenate([pair, pair], axis=1) - energy
            columns = pl.ds(pl.multiple_of(t * WIDTH, WIDTH), WIDTH)
            inv[g * 8:(g + 1) * 8, columns] = jnp.where(keep, 1.0 / denom, 0.0)
        return carry

    lax.fori_loop(0, TILES, tile_body, 0)

    forwards = []
    for i, (dy, dz) in enumerate(BLOCKS):
        blocks[i].wait_recv()
        there = gath.at[0, core, block_rows(-dy, -dz), :]
        forwards.append(send(there, there, fwd_s.at[i], fwd_r.at[i], at(dc=1)))
    spread = []
    for j in range(1, NX):
        spread.append(send(gath.at[0, core], gath.at[j, core], x_s.at[j - 1], x_r.at[j - 1], at(dx=-X_OFF[j])))
    for copy in forwards:
        copy.wait_recv()
    load.wait()

    def multiply(j):
        def body(n, carry):
            rows = pl.ds(pl.multiple_of(n * STEP, STEP), STEP)
            dims = (((1,), (1,)), ((), ()))
            product = lax.dot_general(gath[j, 0], ints[rows, :HALF], dims, preferred_element_type=F32)
            product += lax.dot_general(gath[j, 1], ints[rows, HALF:], dims, preferred_element_type=F32)
            rounded = product.astype(BF16)
            for k in range(NOCC):
                for g in range(2):
                    first = (k * 2 + g) * GROUP
                    part[j, k, g, :, rows] = rounded[first:first + GROUP]
            return carry

        lax.fori_loop(0, ROWS // STEP, body, 0)

    up, down, far = (occ + 1) % NOCC, (occ + 3) % NOCC, (occ + 2) % NOCC
    z = [[None] * 6 for _ in range(NX)]
    mirrors = [None] * NX

    def first_stage(j):
        plan = [
            (part.at[j, far, 0], sum1.at[j, 0], 1),
            (part.at[j, far, 1], sum1.at[j, 1], -1),
            (part.at[j, up, 1], sum2.at[j, 0, 1], 1),
            (part.at[j, down, 0], sum2.at[j, 1, 0], -1),
        ]
        for i, (src, dst, to) in enumerate(plan):
            z[j][i] = send(src, dst, z_s.at[j, i], z_r.at[j, i], at(dh=to))

    def second_stage(j):
        z[j][0].wait_recv()
        part[j, up, 0] = (part[j, up, 0].astype(F32) + sum1[j, 0].astype(F32)).astype(BF16)
        z[j][4] = send(part.at[j, up, 0], sum2.at[j, 0, 0], z_s.at[j, 4], z_r.at[j, 4], at(dh=1))
        z[j][1].wait_recv()
        part[j, down, 1] = (part[j, down, 1].astype(F32) + sum1[j, 1].astype(F32)).astype(BF16)
        z[j][5] = send(part.at[j, down, 1], sum2.at[j, 1, 1], z_s.at[j, 5], z_r.at[j, 5], at(dh=-1))

    def ladder(j):
        for i in range(2, 6):
            z[j][i].wait_recv()
        for g in range(2):
            total = part[j, occ, g].astype(F32) + sum2[j, 0, g].astype(F32) + sum2[j, 1, g].astype(F32)
            outs[j, g] = total
            low[j, g] = total.astype(BF16)
        mirrors[j] = send(low.at[j], mirr.at[j], m_s.at[j], m_r.at[j], at(dy=2))

    stores = []

    def finish(j):
        mirrors[j].wait_recv()
        xx = (x + X_OFF[j] + NX) % NX
        for g in range(2):
            stack = jnp.concatenate([mirr[j, g, :, t * WIDTH:(t + 1) * WIDTH] for t in range(TILES)], axis=0)
            flipped = jnp.dot(stack, perm[...], preferred_element_type=F32)
            rows = pl.ds(pl.multiple_of(g * 64 + xx * GROUP, GROUP), GROUP)
            for t in range(TILES):
                columns = slice(t * WIDTH, (t + 1) * WIDTH)
                total = outs[j, g, :, columns] + flipped[t * GROUP:(t + 1) * GROUP]
                outs[j, g, :, columns] = total * inv[rows, columns]
            store = pltpu.make_async_copy(outs.at[j, g], out_hbm.at[rows, :], store_sem.at[j, g])
            store.start()
            stores.append(store)

    def arrive(j):
        spread[j - 1].wait_recv()
        there = gath.at[j, core]
        send(there, there, xf_s.at[j - 1], xf_r.at[j - 1], at(dc=1)).wait_recv()

    multiply(0)
    first_stage(0)
    arrive(1)
    multiply(1)
    first_stage(1)
    second_stage(0)
    arrive(2)
    multiply(2)
    first_stage(2)
    ladder(0)
    second_stage(1)
    arrive(3)
    multiply(3)
    first_stage(3)
    ladder(1)
    second_stage(2)
    finish(0)
    ladder(2)
    second_stage(3)
    finish(1)
    ladder(3)
    finish(2)
    finish(3)
    for copy in sends:
        copy.wait_send()
    for store in stores:
        store.wait()


def per_device(integrals, amplitudes, tile_list, occ_pairs, e_occ, e_virt):
    dma = pltpu.SemaphoreType.DMA
    any_space = pl.BlockSpec(memory_space=pl.ANY)
    vmem = pl.BlockSpec(memory_space=pltpu.VMEM)
    smem = pl.BlockSpec(memory_space=pltpu.SMEM)
    return pl.pallas_call(
        kernel,
        out_shape=jax.ShapeDtypeStruct((SHARE, ROWS), F32),
        in_specs=[any_space, vmem, smem, smem, smem, smem],
        out_specs=any_space,
        scratch_shapes=[
            pltpu.VMEM((ROWS, CD), BF16),
            pltpu.VMEM((GROUP, CD), BF16),
            pltpu.VMEM((GROUP, CD), BF16),
            pltpu.VMEM((NX, 2, CHUNK, HALF), BF16),
            pltpu.VMEM((NX, NOCC, 2, GROUP, ROWS), BF16),
            pltpu.VMEM((NX, 2, GROUP, ROWS), BF16),
            pltpu.VMEM((NX, 2, 2, GROUP, ROWS), BF16),
            pltpu.VMEM((NX, 2, GROUP, ROWS), BF16),
            pltpu.VMEM((NX, 2, GROUP, ROWS), BF16),
            pltpu.VMEM((NX, 2, GROUP, ROWS), F32),
            pltpu.VMEM((SHARE, ROWS), F32),
            pltpu.VMEM((SHARE, 128), F32),
            pltpu.VMEM((WIDTH, WIDTH), BF16),
            dma,
            dma((NX, 2)),
            dma((2,)),
            dma((len(BLOCKS),)), dma((len(BLOCKS),)),
            dma((len(BLOCKS),)), dma((len(BLOCKS),)),
            dma((NX - 1,)), dma((NX - 1,)),
            dma((NX - 1,)), dma((NX - 1,)),
            dma((NX, 6)), dma((NX, 6)),
            dma((NX,)), dma((NX,)),
        ],
        compiler_params=pltpu.CompilerParams(
            collective_id=0, has_side_effects=True, vmem_limit_bytes=48 << 20
        ),
        cost_estimate=pl.CostEstimate(flops=2 * PAIRS * ROWS * CD, bytes_accessed=10 << 20, transcendentals=0),
    )(integrals, amplitudes, tile_list.T, occ_pairs.T, e_occ, e_virt)


def solution(mesh):
    placed = (P("loop", "occ"), P("loop", "occ"), P("loop", None), P(), P(), P())
    return jax.shard_map(
        per_device, mesh=mesh, in_specs=placed, out_specs=P("occ", "loop"), check_vma=False
    )
```

```python
import jax
import jax.numpy as jnp
from jax import lax
from jax.experimental import pallas as pl
from jax.experimental.pallas import tpu as pltpu
from jax.sharding import PartitionSpec as P

MESH = pl.DeviceIdType.MESH
TILE = 16
WIDTH = TILE * TILE
ROWS = 2048
TILES = ROWS // WIDTH
CD = 2048
HALF = 1024
QUARTER = 512
PAIRS = 512
SHARE = 128
NY, NZL, NX, NCORE, NOCC = 4, 2, 4, 2, 4
CHIPS = NY * NZL
CHUNK = 128
GROUP = 16
X_OFF = (0, 1, -1, 2)
BLOCKS = [(dy, dz) for dy in (0, 1, 3, 2) for dz in range(NZL)][1:]
BF16, F32 = jnp.bfloat16, jnp.float32


def kernel(
    ints_hbm, amps_hbm, tiles_hbm, pairs_hbm, e_occ_hbm, e_virt_hbm, out,
    ints, amps, tiles, pairs, e_occ, e_virt, gath, left,
    part_a, sum1_a, sum2_a, low_a, mirr_a,
    part_b, mirr_b, sum1_b, sum2_b, back_b, done_b,
    inv, pair_e, perm,
    load_sem, blk_s, blk_r, fwd_s, fwd_r, x_s, x_r, x3_s, x3_r, xf_s, xf_r, za_s, za_r, zb_s, zb_r, y_s, y_r,
):
    loop, occ = lax.axis_index("loop"), lax.axis_index("occ")
    core, x, zl, y = loop % 2, (loop // 2) % NX, (loop // 8) % NZL, loop // 16
    half = y // 2

    def at(dy=0, dz=0, dx=0, dc=0, dh=0):
        yy, zz = (y + dy + NY) % NY, (zl + dz) % NZL
        xx, cc = (x + dx + NX) % NX, (core + dc) % NCORE
        return ((yy * NZL + zz) * NX + xx) * NCORE + cc, (occ + dh + NOCC) % NOCC

    sends = []

    def send(src, dst, send_sem, recv_sem, to):
        copy = pltpu.make_async_remote_copy(
            src_ref=src, dst_ref=dst, send_sem=send_sem, recv_sem=recv_sem,
            device_id=to, device_id_type=MESH,
        )
        copy.start()
        sends.append(copy)
        return copy

    partners = [at(dc=1), at(dh=1), at(dh=-1)]
    partners += [at(dx=d) for d in X_OFF[1:]]
    partners += [at(dy=dy, dz=dz) for dy, dz in BLOCKS]
    barrier = pltpu.get_barrier_semaphore()
    for partner in partners:
        pl.semaphore_signal(barrier, inc=1, device_id=partner, device_id_type=MESH)
    loads = []
    for i, (src, dst) in enumerate((
        (amps_hbm, amps), (tiles_hbm, tiles), (pairs_hbm, pairs),
        (e_occ_hbm, e_occ), (e_virt_hbm, e_virt), (ints_hbm, ints),
    )):
        loads.append(pltpu.make_async_copy(src, dst, load_sem.at[i]))
        loads[-1].start()
    loads[0].wait()

    def block_at(dy, dz):
        return ((y + dy + NY) % NY) * NZL + (zl + dz) % NZL

    here = block_at(0, 0)
    rows8 = amps[...].astype(F32)
    gath[0, core, here] = jnp.concatenate([rows8[:, :HALF], rows8[:, HALF:]], axis=0).astype(BF16)
    pl.semaphore_wait(barrier, len(partners))

    def hand_on(i, block):
        forwards.append(send(block, block, fwd_s.at[i], fwd_r.at[i], at(dc=1)))

    def step_x(i, index):
        for j in (1, 2):
            copy = send(
                gath.at[0, core, index], gath.at[j, core, index], x_s.at[j - 1, i], x_r.at[j - 1, i], at(dx=-X_OFF[j])
            )
            chunks[j].append(copy)

    mine = gath.at[0, core, here]
    blocks, forwards, chunks = [], [], [[] for _ in range(NX)]
    for i, (dy, dz) in enumerate(BLOCKS):
        blocks.append(send(mine, mine, blk_s.at[i], blk_r.at[i], at(dy=dy, dz=dz)))
    hand_on(len(BLOCKS), mine)
    step_x(len(BLOCKS), here)
    for i, (dy, dz) in enumerate(BLOCKS):
        blocks[i].wait_recv()
        there = block_at(-dy, -dz)
        hand_on(i, gath.at[0, core, there])
        step_x(i, there)

    def spread_far():
        chunks[3].append(send(gath.at[0, core], gath.at[3, core], x3_s.at[0], x3_r.at[0], at(dx=-X_OFF[3])))

    def merge(j):
        for b in range(CHIPS):
            for h in range(2):
                lower = gath[j, 0, b].astype(F32)[8 * h:8 * h + 8]
                upper = gath[j, 1, b].astype(F32)[8 * h:8 * h + 8]
                left[h, b * GROUP:(b + 1) * GROUP, :] = jnp.concatenate([lower, upper], axis=0).astype(BF16)

    def multiply(second):
        dims = (((1,), (1,)), ((), ()))
        rows = slice(second * HALF, (second + 1) * HALF)
        product = lax.dot_general(left[0], ints[rows, :HALF], dims, preferred_element_type=F32)
        product += lax.dot_general(left[1], ints[rows, HALF:], dims, preferred_element_type=F32)
        rounded = product.astype(BF16)
        return [rounded[i * GROUP:(i + 1) * GROUP] for i in range(CHIPS)]

    def flip(blocks):
        stack = jnp.concatenate(
            [block[:, t * WIDTH:(t + 1) * WIDTH] for block in blocks for t in range(HALF // WIDTH)], axis=0
        )
        flipped = jnp.dot(stack, perm[...], preferred_element_type=F32)
        parts = [flipped[i * GROUP:(i + 1) * GROUP] for i in range(len(blocks) * (HALF // WIDTH))]
        n = HALF // WIDTH
        return [jnp.concatenate(parts[i * n:(i + 1) * n], axis=1) for i in range(len(blocks))]

    up, down, far = (occ + 1) % NOCC, (occ + 3) % NOCC, (occ + 2) % NOCC
    za = [[None] * 6 for _ in range(NX)]
    zb = [[None] * 6 for _ in range(NX)]
    ys = [[None] * 3 for _ in range(NX)]

    def out_rows(j, g):
        xx = (x + X_OFF[j] + NX) % NX
        return pl.ds(pl.multiple_of(g * 64 + xx * GROUP, GROUP), GROUP)

    def product_b(j):
        for i, block in enumerate(multiply(1)):
            part_b[j, i % 2, i // 2] = block
        ys[j][0] = send(part_b.at[j, 1 - half], mirr_b.at[j], y_s.at[j, 0], y_r.at[j, 0], at(dy=2))

    def first_b(j):
        ys[j][0].wait_recv()
        flipped = flip([mirr_b[j, k] for k in range(NOCC)])
        for k in range(NOCC):
            part_b[j, half, k] = (part_b[j, half, k].astype(F32) + flipped[k]).astype(BF16)
        plan = [
            (part_b.at[j, half, far, :, :QUARTER], sum1_b.at[j, 0], 1),
            (part_b.at[j, half, far, :, QUARTER:], sum1_b.at[j, 1], -1),
            (part_b.at[j, half, up, :, QUARTER:], sum2_b.at[j, 0, 1], 1),
            (part_b.at[j, half, down, :, :QUARTER], sum2_b.at[j, 1, 0], -1),
        ]
        for i, (src, dst, to) in enumerate(plan):
            zb[j][i] = send(src, dst, zb_s.at[j, i], zb_r.at[j, i], at(dh=to))

    def second_b(j):
        for i, who, columns, to in ((0, up, slice(0, QUARTER), 1), (1, down, slice(QUARTER, HALF), -1)):
            zb[j][i].wait_recv()
            total = part_b[j, half, who, :, columns].astype(F32) + sum1_b[j, i].astype(F32)
            part_b[j, half, who, :, columns] = total.astype(BF16)
            zb[j][4 + i] = send(
                part_b.at[j, half, who, :, columns], sum2_b.at[j, i, i], zb_s.at[j, 4 + i], zb_r.at[j, 4 + i], at(dh=to)
            )

    def total_b(j):
        for i in range(2, 6):
            zb[j][i].wait_recv()
        both = [jnp.concatenate([sum2_b[j, i, 0], sum2_b[j, i, 1]], axis=1).astype(F32) for i in range(2)]
        total = part_b[j, half, occ].astype(F32) + both[0] + both[1]
        back_b[j] = total.astype(BF16)
        ys[j][2] = send(back_b.at[j], done_b.at[j], y_s.at[j, 2], y_r.at[j, 2], at(dy=2))
        rows = out_rows(j, half)
        out[rows, HALF:] = total * inv[rows, HALF:]

    def finish_b(j):
        ys[j][2].wait_recv()
        rows = out_rows(j, 1 - half)
        out[rows, HALF:] = flip([done_b[j]])[0] * inv[rows, HALF:]

    def product_a(j):
        for i, block in enumerate(multiply(0)):
            part_a[j, i // 2, i % 2] = block
        plan = [
            (part_a.at[j, far, 0], sum1_a.at[j, 0], 1),
            (part_a.at[j, far, 1], sum1_a.at[j, 1], -1),
            (part_a.at[j, up, 1], sum2_a.at[j, 0, 1], 1),
            (part_a.at[j, down, 0], sum2_a.at[j, 1, 0], -1),
        ]
        for i, (src, dst, to) in enumerate(plan):
            za[j][i] = send(src, dst, za_s.at[j, i], za_r.at[j, i], at(dh=to))

    def second_a(j):
        for i, who, to in ((0, up, 1), (1, down, -1)):
            za[j][i].wait_recv()
            part_a[j, who, i] = (part_a[j, who, i].astype(F32) + sum1_a[j, i].astype(F32)).astype(BF16)
            za[j][4 + i] = send(part_a.at[j, who, i], sum2_a.at[j, i, i], za_s.at[j, 4 + i], za_r.at[j, 4 + i], at(dh=to))

    def total_a(j):
        for i in range(2, 6):
            za[j][i].wait_recv()
        for g in range(2):
            total = part_a[j, occ, g].astype(F32) + sum2_a[j, 0, g].astype(F32) + sum2_a[j, 1, g].astype(F32)
            out[out_rows(j, g), :HALF] = total
            low_a[j, g] = total.astype(BF16)
        ys[j][1] = send(low_a.at[j], mirr_a.at[j], y_s.at[j, 1], y_r.at[j, 1], at(dy=2))

    def finish_a(j):
        ys[j][1].wait_recv()
        flipped = flip([mirr_a[j, g] for g in range(2)])
        for g in range(2):
            rows = out_rows(j, g)
            out[rows, :HALF] = (out[rows, :HALF] + flipped[g]) * inv[rows, :HALF]

    siblings = [None] * NX

    def pass_on(j):
        for copy in chunks[j]:
            copy.wait_recv()
        there = gath.at[j, core]
        siblings[j] = send(there, there, xf_s.at[j - 1], xf_r.at[j - 1], at(dc=1))

    def arrive(j):
        siblings[j].wait_recv()
        merge(j)

    def energies():
        for load in loads[1:5]:
            load.wait()
        sub = lax.broadcasted_iota(jnp.int32, (8, 128), 0)

        def pair_body(g, carry):
            rows = jnp.zeros((8, 128), F32)
            for i in range(8):
                pair = occ * SHARE + g * 8 + i
                energy = e_occ[pairs[0, pair]] + e_occ[pairs[1, pair]]
                rows = jnp.where(sub == i, energy, rows)
            pair_e[pl.ds(pl.multiple_of(g * 8, 8), 8), :] = rows
            return carry

        lax.fori_loop(0, SHARE // 8, pair_body, 0)
        lane = lax.broadcasted_iota(jnp.int32, (8, WIDTH), 1)
        lane_x, lane_y = lane // TILE, lane % TILE

        def tile_body(t, carry):
            first, second = tiles[0, t], tiles[1, t]
            a, b = jnp.maximum(first, 0) * TILE, jnp.maximum(second, 0) * TILE
            e_a = jnp.zeros((8, WIDTH), F32)
            e_b = jnp.zeros((8, WIDTH), F32)
            for i in range(TILE):
                e_a = jnp.where(lane_x == i, e_virt[a + i], e_a)
                e_b = jnp.where(lane_y == i, e_virt[b + i], e_b)
            energy = e_a + e_b
            keep = jnp.full((8, WIDTH), first, jnp.int32) >= 0
            columns = pl.ds(pl.multiple_of(t * WIDTH, WIDTH), WIDTH)
            for g in range(SHARE // 8):
                pair = pair_e[g * 8:(g + 1) * 8, :]
                denom = jnp.concatenate([pair, pair], axis=1) - energy
                inv[g * 8:(g + 1) * 8, columns] = jnp.where(keep, 1.0 / denom, 0.0)
            return carry

        lax.fori_loop(0, TILES, tile_body, 0)

    row_at = lax.broadcasted_iota(jnp.int32, (WIDTH, WIDTH), 0)
    col_at = lax.broadcasted_iota(jnp.int32, (WIDTH, WIDTH), 1)
    perm[...] = jnp.where(col_at == (row_at % TILE) * TILE + row_at // TILE, 1.0, 0.0).astype(BF16)
    for copy in forwards:
        copy.wait_recv()
    merge(0)
    loads[5].wait()
    product_b(0)
    product_a(0)
    spread_far()
    pass_on(1)
    energies()
    arrive(1)
    product_b(1)
    pass_on(2)
    product_a(1)
    first_b(0)
    second_a(0)
    arrive(2)
    product_b(2)
    pass_on(3)
    product_a(2)
    second_b(0)
    total_a(0)
    first_b(1)
    second_a(1)
    arrive(3)
    product_b(3)
    product_a(3)
    total_b(0)
    finish_a(0)
    second_b(1)
    total_a(1)
    first_b(2)
    second_a(2)
    finish_b(0)
    total_b(1)
    finish_a(1)
    second_b(2)
    total_a(2)
    first_b(3)
    second_a(3)
    finish_b(1)
    total_b(2)
    finish_a(2)
    second_b(3)
    total_a(3)
    finish_b(2)
    total_b(3)
    finish_a(3)
    finish_b(3)
    for copy in sends:
        copy.wait_send()


def per_device(integrals, amplitudes, tile_list, occ_pairs, e_occ, e_virt):
    dma = pltpu.SemaphoreType.DMA
    vmem, smem = pltpu.VMEM, pltpu.SMEM
    n_blocks = len(BLOCKS)
    operands = integrals, amplitudes, tile_list.T, occ_pairs.T, e_occ, e_virt
    operands = [pltpu.with_memory_space_constraint(operand, pltpu.HBM) for operand in operands]
    return pl.pallas_call(
        kernel,
        out_shape=jax.ShapeDtypeStruct((SHARE, ROWS), F32),
        in_specs=[pl.BlockSpec(memory_space=pltpu.HBM)] * 6,
        out_specs=pl.BlockSpec(memory_space=vmem),
        scratch_shapes=[
            vmem((ROWS, CD), BF16),
            vmem((8, CD), BF16),
            smem((2, TILES), jnp.int32),
            smem((2, PAIRS), jnp.int32),
            smem(e_occ.shape, F32),
            smem(e_virt.shape, F32),
            vmem((NX, NCORE, CHIPS, GROUP, HALF), BF16),
            vmem((2, CHUNK, HALF), BF16),
            vmem((NX, NOCC, 2, GROUP, HALF), BF16),
            vmem((NX, 2, GROUP, HALF), BF16),
            vmem((NX, 2, 2, GROUP, HALF), BF16),
            vmem((NX, 2, GROUP, HALF), BF16),
            vmem((NX, 2, GROUP, HALF), BF16),
            vmem((NX, 2, NOCC, GROUP, HALF), BF16),
            vmem((NX, NOCC, GROUP, HALF), BF16),
            vmem((NX, 2, GROUP, QUARTER), BF16),
            vmem((NX, 2, 2, GROUP, QUARTER), BF16),
            vmem((NX, GROUP, HALF), BF16),
            vmem((NX, GROUP, HALF), BF16),
            vmem((SHARE, ROWS), F32),
            vmem((SHARE, 128), F32),
            vmem((WIDTH, WIDTH), BF16),
            dma((6,)),
            dma((n_blocks,)), dma((n_blocks,)),
            dma((n_blocks + 1,)), dma((n_blocks + 1,)),
            dma((2, n_blocks + 1)), dma((2, n_blocks + 1)),
            dma((1,)), dma((1,)),
            dma((NX - 1,)), dma((NX - 1,)),
            dma((NX, 6)), dma((NX, 6)),
            dma((NX, 6)), dma((NX, 6)),
            dma((NX, 3)), dma((NX, 3)),
        ],
        compiler_params=pltpu.CompilerParams(
            collective_id=0, has_side_effects=True, vmem_limit_bytes=48 << 20
        ),
        cost_estimate=pl.CostEstimate(flops=2 * PAIRS * ROWS * CD, bytes_accessed=10 << 20, transcendentals=0),
    )(*operands)


def solution(mesh):
    placed = (P("loop", "occ"), P("loop", "occ"), P("loop", None), P(), P(), P())
    return jax.shard_map(
        per_device, mesh=mesh, in_specs=placed, out_specs=P("occ", "loop"), check_vma=False
    )
```

```python
import jax
import jax.numpy as jnp
from jax import lax
from jax.experimental import pallas as pl
from jax.experimental.pallas import tpu as pltpu
from jax.sharding import PartitionSpec as P

MESH = pl.DeviceIdType.MESH
TILE = 16
WIDTH = TILE * TILE
ROWS = 2048
TILES = ROWS // WIDTH
CD = 2048
HALF = 1024
COLS_A = 3 * WIDTH
COLS_B = ROWS - COLS_A
MID = COLS_B // 2
PAIRS = 512
SHARE = 128
NY, NZL, NX, NCORE, NOCC = 4, 2, 4, 2, 4
CHIPS = NY * NZL
CHUNK = 128
GROUP = 16
X_OFF = (0, 1, -1, 2)
BLOCKS = [(dy, dz) for dy in (0, 1, 3, 2) for dz in range(NZL)][1:]
BF16, F32 = jnp.bfloat16, jnp.float32


def kernel(
    ints_hbm, amps_hbm, tiles_hbm, pairs_hbm, e_occ_hbm, e_virt_hbm, out,
    ints, amps, tiles, pairs, e_occ, e_virt, gath, left,
    part_a, sum1_a, sum2_a, low_a, mirr_a,
    part_b, mirr_b, sum1_b, sum2_b, back_b, done_b,
    inv, pair_e, perm,
    load_sem, blk_s, blk_r, fwd_s, fwd_r, x_s, x_r, x3_s, x3_r, xf_s, xf_r, za_s, za_r, zb_s, zb_r, y_s, y_r,
):
    loop, occ = lax.axis_index("loop"), lax.axis_index("occ")
    core, x, zl, y = loop % 2, (loop // 2) % NX, (loop // 8) % NZL, loop // 16
    half = y // 2

    def at(dy=0, dz=0, dx=0, dc=0, dh=0):
        yy, zz = (y + dy + NY) % NY, (zl + dz) % NZL
        xx, cc = (x + dx + NX) % NX, (core + dc) % NCORE
        return ((yy * NZL + zz) * NX + xx) * NCORE + cc, (occ + dh + NOCC) % NOCC

    sends = []

    def send(src, dst, send_sem, recv_sem, to):
        copy = pltpu.make_async_remote_copy(
            src_ref=src, dst_ref=dst, send_sem=send_sem, recv_sem=recv_sem,
            device_id=to, device_id_type=MESH,
        )
        copy.start()
        sends.append(copy)
        return copy

    partners = [at(dc=1), at(dh=1), at(dh=-1)]
    partners += [at(dx=1), at(dx=-1)]
    partners += [at(dy=dy, dz=dz) for dy, dz in BLOCKS]
    barrier = pltpu.get_barrier_semaphore()
    for partner in partners:
        pl.semaphore_signal(barrier, inc=1, device_id=partner, device_id_type=MESH)
    loads = []
    for i, (src, dst) in enumerate((
        (amps_hbm, amps), (tiles_hbm, tiles), (pairs_hbm, pairs),
        (e_occ_hbm, e_occ), (e_virt_hbm, e_virt), (ints_hbm, ints),
    )):
        loads.append(pltpu.make_async_copy(src, dst, load_sem.at[i]))
        loads[-1].start()
    loads[0].wait()

    def block_at(dy, dz):
        return ((y + dy + NY) % NY) * NZL + (zl + dz) % NZL

    here = block_at(0, 0)
    rows8 = amps[...].astype(F32)
    gath[0, core, here] = jnp.concatenate([rows8[:, :HALF], rows8[:, HALF:]], axis=0).astype(BF16)
    pl.semaphore_wait(barrier, len(partners))

    def hand_on(i, block):
        forwards.append(send(block, block, fwd_s.at[i], fwd_r.at[i], at(dc=1)))

    def step_x(i, index):
        for j in (1, 2):
            copy = send(
                gath.at[0, core, index], gath.at[j, core, index], x_s.at[j - 1, i], x_r.at[j - 1, i], at(dx=-X_OFF[j])
            )
            chunks[j].append(copy)

    mine = gath.at[0, core, here]
    blocks, forwards, chunks = [], [], [[] for _ in range(NX)]
    for i, (dy, dz) in enumerate(BLOCKS):
        blocks.append(send(mine, mine, blk_s.at[i], blk_r.at[i], at(dy=dy, dz=dz)))
    hand_on(len(BLOCKS), mine)
    step_x(len(BLOCKS), here)
    for i, (dy, dz) in enumerate(BLOCKS):
        blocks[i].wait_recv()
        there = block_at(-dy, -dz)
        hand_on(i, gath.at[0, core, there])
        step_x(i, there)

    def relay():
        part = slice(0, CHIPS // 2)
        chunks[3].append(send(gath.at[1, core, part], gath.at[3, core, part], x3_s.at[0], x3_r.at[0], at(dx=-1)))
        part = slice(CHIPS // 2, CHIPS)
        chunks[3].append(send(gath.at[2, core, part], gath.at[3, core, part], x3_s.at[1], x3_r.at[1], at(dx=1)))

    def merge(j, slot):
        for b in range(CHIPS):
            for h in range(2):
                lower = gath[j, 0, b].astype(F32)[8 * h:8 * h + 8]
                upper = gath[j, 1, b].astype(F32)[8 * h:8 * h + 8]
                rows = slice(slot * CHUNK + b * GROUP, slot * CHUNK + (b + 1) * GROUP)
                left[h, rows, :] = jnp.concatenate([lower, upper], axis=0).astype(BF16)

    def multiply(rows, chunks):
        dims = (((1,), (1,)), ((), ()))
        here = slice(0, chunks * CHUNK)
        product = lax.dot_general(left[0, here], ints[rows, :HALF], dims, preferred_element_type=F32)
        product += lax.dot_general(left[1, here], ints[rows, HALF:], dims, preferred_element_type=F32)
        rounded = product.astype(BF16)
        return [rounded[i * GROUP:(i + 1) * GROUP] for i in range(chunks * CHIPS)]

    def flip(blocks):
        n = blocks[0].shape[1] // WIDTH
        stack = jnp.concatenate([block[:, t * WIDTH:(t + 1) * WIDTH] for block in blocks for t in range(n)], axis=0)
        flipped = jnp.dot(stack, perm[...], preferred_element_type=F32)
        parts = [flipped[i * GROUP:(i + 1) * GROUP] for i in range(len(blocks) * n)]
        return [jnp.concatenate(parts[i * n:(i + 1) * n], axis=1) for i in range(len(blocks))]

    up, down, far = (occ + 1) % NOCC, (occ + 3) % NOCC, (occ + 2) % NOCC
    za = [[None] * 6 for _ in range(NX)]
    zb = [[None] * 6 for _ in range(NX)]
    ys = [[None] * 3 for _ in range(NX)]

    def out_rows(j, g):
        xx = (x + X_OFF[j] + NX) % NX
        return pl.ds(pl.multiple_of(g * 64 + xx * GROUP, GROUP), GROUP)

    def product_b(*js):
        found = multiply(slice(COLS_A, ROWS), len(js))
        for n, j in enumerate(js):
            for i in range(CHIPS):
                part_b[j, i % 2, i // 2] = found[n * CHIPS + i]
            ys[j][0] = send(part_b.at[j, 1 - half], mirr_b.at[j], y_s.at[j, 0], y_r.at[j, 0], at(dy=2))

    def first_b(j):
        ys[j][0].wait_recv()
        flipped = flip([mirr_b[j, k] for k in range(NOCC)])
        for k in range(NOCC):
            part_b[j, half, k] = (part_b[j, half, k].astype(F32) + flipped[k]).astype(BF16)
        plan = [
            (part_b.at[j, half, far, :, :MID], sum1_b.at[j, 0], 1),
            (part_b.at[j, half, far, :, MID:], sum1_b.at[j, 1], -1),
            (part_b.at[j, half, up, :, MID:], sum2_b.at[j, 0, 1], 1),
            (part_b.at[j, half, down, :, :MID], sum2_b.at[j, 1, 0], -1),
        ]
        for i, (src, dst, to) in enumerate(plan):
            zb[j][i] = send(src, dst, zb_s.at[j, i], zb_r.at[j, i], at(dh=to))

    def second_b(j):
        for i, who, columns, to in ((0, up, slice(0, MID), 1), (1, down, slice(MID, COLS_B), -1)):
            zb[j][i].wait_recv()
            total = part_b[j, half, who, :, columns].astype(F32) + sum1_b[j, i].astype(F32)
            part_b[j, half, who, :, columns] = total.astype(BF16)
            zb[j][4 + i] = send(
                part_b.at[j, half, who, :, columns], sum2_b.at[j, i, i], zb_s.at[j, 4 + i], zb_r.at[j, 4 + i], at(dh=to)
            )

    def total_b(j):
        for i in range(2, 6):
            zb[j][i].wait_recv()
        both = [jnp.concatenate([sum2_b[j, i, 0], sum2_b[j, i, 1]], axis=1).astype(F32) for i in range(2)]
        total = part_b[j, half, occ].astype(F32) + both[0] + both[1]
        back_b[j] = total.astype(BF16)
        ys[j][2] = send(back_b.at[j], done_b.at[j], y_s.at[j, 2], y_r.at[j, 2], at(dy=2))
        rows = out_rows(j, half)
        out[rows, COLS_A:] = total * inv[rows, COLS_A:]

    def finish_b(j):
        ys[j][2].wait_recv()
        rows = out_rows(j, 1 - half)
        out[rows, COLS_A:] = flip([done_b[j]])[0] * inv[rows, COLS_A:]

    def product_a(*js):
        found = multiply(slice(0, COLS_A), len(js))
        for n, j in enumerate(js):
            for i in range(CHIPS):
                part_a[j, i // 2, i % 2] = found[n * CHIPS + i]
            plan = [
                (part_a.at[j, far, 0], sum1_a.at[j, 0], 1),
                (part_a.at[j, far, 1], sum1_a.at[j, 1], -1),
                (part_a.at[j, up, 1], sum2_a.at[j, 0, 1], 1),
                (part_a.at[j, down, 0], sum2_a.at[j, 1, 0], -1),
            ]
            for i, (src, dst, to) in enumerate(plan):
                za[j][i] = send(src, dst, za_s.at[j, i], za_r.at[j, i], at(dh=to))

    def second_a(j):
        for i, who, to in ((0, up, 1), (1, down, -1)):
            za[j][i].wait_recv()
            part_a[j, who, i] = (part_a[j, who, i].astype(F32) + sum1_a[j, i].astype(F32)).astype(BF16)
            za[j][4 + i] = send(part_a.at[j, who, i], sum2_a.at[j, i, i], za_s.at[j, 4 + i], za_r.at[j, 4 + i], at(dh=to))

    def total_a(j):
        for i in range(2, 6):
            za[j][i].wait_recv()
        for g in range(2):
            total = part_a[j, occ, g].astype(F32) + sum2_a[j, 0, g].astype(F32) + sum2_a[j, 1, g].astype(F32)
            out[out_rows(j, g), :COLS_A] = total
            low_a[j, g] = total.astype(BF16)
        ys[j][1] = send(low_a.at[j], mirr_a.at[j], y_s.at[j, 1], y_r.at[j, 1], at(dy=2))

    def finish_a(j):
        ys[j][1].wait_recv()
        flipped = flip([mirr_a[j, g] for g in range(2)])
        for g in range(2):
            rows = out_rows(j, g)
            out[rows, :COLS_A] = (out[rows, :COLS_A] + flipped[g]) * inv[rows, :COLS_A]

    siblings = [None] * NX

    def pass_on(j):
        for copy in chunks[j]:
            copy.wait_recv()
        there = gath.at[j, core]
        siblings[j] = send(there, there, xf_s.at[j - 1], xf_r.at[j - 1], at(dc=1))

    def arrive(j, slot):
        siblings[j].wait_recv()
        merge(j, slot)

    def energies():
        for load in loads[1:5]:
            load.wait()
        sub = lax.broadcasted_iota(jnp.int32, (8, 128), 0)

        def pair_body(g, carry):
            rows = jnp.zeros((8, 128), F32)
            for i in range(8):
                pair = occ * SHARE + g * 8 + i
                energy = e_occ[pairs[0, pair]] + e_occ[pairs[1, pair]]
                rows = jnp.where(sub == i, energy, rows)
            pair_e[pl.ds(pl.multiple_of(g * 8, 8), 8), :] = rows
            return carry

        lax.fori_loop(0, SHARE // 8, pair_body, 0)
        lane = lax.broadcasted_iota(jnp.int32, (8, WIDTH), 1)
        lane_x, lane_y = lane // TILE, lane % TILE

        def tile_body(t, carry):
            first, second = tiles[0, t], tiles[1, t]
            a, b = jnp.maximum(first, 0) * TILE, jnp.maximum(second, 0) * TILE
            e_a = jnp.zeros((8, WIDTH), F32)
            e_b = jnp.zeros((8, WIDTH), F32)
            for i in range(TILE):
                e_a = jnp.where(lane_x == i, e_virt[a + i], e_a)
                e_b = jnp.where(lane_y == i, e_virt[b + i], e_b)
            energy = e_a + e_b
            keep = jnp.full((8, WIDTH), first, jnp.int32) >= 0
            columns = pl.ds(pl.multiple_of(t * WIDTH, WIDTH), WIDTH)
            for g in range(SHARE // 8):
                pair = pair_e[g * 8:(g + 1) * 8, :]
                denom = jnp.concatenate([pair, pair], axis=1) - energy
                inv[g * 8:(g + 1) * 8, columns] = jnp.where(keep, 1.0 / denom, 0.0)
            return carry

        lax.fori_loop(0, TILES, tile_body, 0)

    row_at = lax.broadcasted_iota(jnp.int32, (WIDTH, WIDTH), 0)
    col_at = lax.broadcasted_iota(jnp.int32, (WIDTH, WIDTH), 1)
    perm[...] = jnp.where(col_at == (row_at % TILE) * TILE + row_at // TILE, 1.0, 0.0).astype(BF16)
    for copy in forwards:
        copy.wait_recv()
    merge(0, 0)
    loads[5].wait()
    product_a(0)
    pass_on(1)
    product_b(0)
    pass_on(2)
    relay()
    arrive(1, 0)
    product_a(1)
    second_a(0)
    product_b(1)
    first_b(0)
    arrive(2, 0)
    product_a(2)
    second_a(1)
    product_b(2)
    pass_on(3)
    first_b(1)
    arrive(3, 0)
    product_a(3)
    second_a(2)
    product_b(3)
    energies()
    second_b(0)
    total_a(0)
    first_b(2)
    second_a(3)
    total_a(1)
    second_b(1)
    first_b(3)
    total_a(2)
    total_b(0)
    second_b(2)
    finish_a(0)
    total_a(3)
    total_b(1)
    second_b(3)
    finish_a(1)
    finish_b(0)
    total_b(2)
    finish_a(2)
    finish_b(1)
    finish_a(3)
    total_b(3)
    finish_b(2)
    finish_b(3)
    for copy in sends:
        copy.wait_send()


def per_device(integrals, amplitudes, tile_list, occ_pairs, e_occ, e_virt):
    dma = pltpu.SemaphoreType.DMA
    vmem, smem = pltpu.VMEM, pltpu.SMEM
    n_blocks = len(BLOCKS)
    operands = integrals, amplitudes, tile_list.T, occ_pairs.T, e_occ, e_virt
    operands = [pltpu.with_memory_space_constraint(operand, pltpu.HBM) for operand in operands]
    return pl.pallas_call(
        kernel,
        out_shape=jax.ShapeDtypeStruct((SHARE, ROWS), F32),
        in_specs=[pl.BlockSpec(memory_space=pltpu.HBM)] * 6,
        out_specs=pl.BlockSpec(memory_space=vmem),
        scratch_shapes=[
            vmem((ROWS, CD), BF16),
            vmem((8, CD), BF16),
            smem((2, TILES), jnp.int32),
            smem((2, PAIRS), jnp.int32),
            smem(e_occ.shape, F32),
            smem(e_virt.shape, F32),
            vmem((NX, NCORE, CHIPS, GROUP, HALF), BF16),
            vmem((2, 2 * CHUNK, HALF), BF16),
            vmem((NX, NOCC, 2, GROUP, COLS_A), BF16),
            vmem((NX, 2, GROUP, COLS_A), BF16),
            vmem((NX, 2, 2, GROUP, COLS_A), BF16),
            vmem((NX, 2, GROUP, COLS_A), BF16),
            vmem((NX, 2, GROUP, COLS_A), BF16),
            vmem((NX, 2, NOCC, GROUP, COLS_B), BF16),
            vmem((NX, NOCC, GROUP, COLS_B), BF16),
            vmem((NX, 2, GROUP, MID), BF16),
            vmem((NX, 2, 2, GROUP, MID), BF16),
            vmem((NX, GROUP, COLS_B), BF16),
            vmem((NX, GROUP, COLS_B), BF16),
            vmem((SHARE, ROWS), F32),
            vmem((SHARE, 128), F32),
            vmem((WIDTH, WIDTH), BF16),
            dma((6,)),
            dma((n_blocks,)), dma((n_blocks,)),
            dma((n_blocks + 1,)), dma((n_blocks + 1,)),
            dma((2, n_blocks + 1)), dma((2, n_blocks + 1)),
            dma((2,)), dma((2,)),
            dma((NX - 1,)), dma((NX - 1,)),
            dma((NX, 6)), dma((NX, 6)),
            dma((NX, 6)), dma((NX, 6)),
            dma((NX, 3)), dma((NX, 3)),
        ],
        compiler_params=pltpu.CompilerParams(
            collective_id=0, has_side_effects=True, vmem_limit_bytes=48 << 20
        ),
        cost_estimate=pl.CostEstimate(flops=2 * PAIRS * ROWS * CD, bytes_accessed=10 << 20, transcendentals=0),
    )(*operands)


def solution(mesh):
    placed = (P("loop", "occ"), P("loop", "occ"), P("loop", None), P(), P(), P())
    return jax.shard_map(
        per_device, mesh=mesh, in_specs=placed, out_specs=P("occ", "loop"), check_vma=False
    )
```

```python
import jax
import jax.numpy as jnp
from jax import lax
from jax.experimental import pallas as pl
from jax.experimental.pallas import tpu as pltpu
from jax.sharding import PartitionSpec as P

MESH = pl.DeviceIdType.MESH
TILE = 16
WIDTH = TILE * TILE
ROWS = 2048
TILES = ROWS // WIDTH
CD = 2048
HALF = 1024
COLS_A = 3 * WIDTH
COLS_B = ROWS - COLS_A
MID = COLS_B // 2
PAIRS = 512
SHARE = 128
NY, NZL, NX, NCORE, NOCC = 4, 2, 4, 2, 4
CHIPS = NY * NZL
CHUNK = 128
GROUP = 16
X_OFF = (0, 1, -1, 2)
BLOCKS = [(dy, dz) for dy in (0, 1, 3, 2) for dz in range(NZL)][1:]
BF16, F32 = jnp.bfloat16, jnp.float32


def kernel(
    ints_hbm, amps_hbm, tiles_hbm, pairs_hbm, e_occ_hbm, e_virt_hbm, out,
    ints, amps, tiles, pairs, e_occ, e_virt, gath, left,
    part_a, sum1_a, sum2_a, low_a, mirr_a,
    part_b, mirr_b, sum1_b, sum2_b, back_b, done_b,
    inv, pair_e, perm,
    load_sem, blk_s, blk_r, fwd_s, fwd_r, x_s, x_r, x3_s, x3_r, xf_s, xf_r, za_s, za_r, zb_s, zb_r, y_s, y_r,
):
    loop, occ = lax.axis_index("loop"), lax.axis_index("occ")
    core, x, zl, y = loop % 2, (loop // 2) % NX, (loop // 8) % NZL, loop // 16
    half = y // 2

    def at(dy=0, dz=0, dx=0, dc=0, dh=0):
        yy, zz = (y + dy + NY) % NY, (zl + dz) % NZL
        xx, cc = (x + dx + NX) % NX, (core + dc) % NCORE
        return ((yy * NZL + zz) * NX + xx) * NCORE + cc, (occ + dh + NOCC) % NOCC

    sends = []

    def send(src, dst, send_sem, recv_sem, to):
        copy = pltpu.make_async_remote_copy(
            src_ref=src, dst_ref=dst, send_sem=send_sem, recv_sem=recv_sem,
            device_id=to, device_id_type=MESH,
        )
        copy.start()
        sends.append(copy)
        return copy

    loads = []
    for i, (src, dst) in enumerate((
        (amps_hbm, amps), (tiles_hbm, tiles), (pairs_hbm, pairs),
        (e_occ_hbm, e_occ), (e_virt_hbm, e_virt), (ints_hbm, ints),
    )):
        loads.append(pltpu.make_async_copy(src, dst, load_sem.at[i]))
        loads[-1].start()
    partners = [at(dc=1), at(dh=1), at(dh=-1)]
    partners += [at(dx=1), at(dx=-1)]
    partners += [at(dy=dy, dz=dz) for dy, dz in BLOCKS]
    barrier = pltpu.get_barrier_semaphore()
    for partner in partners:
        pl.semaphore_signal(barrier, inc=1, device_id=partner, device_id_type=MESH)
    loads[0].wait()

    def block_at(dy, dz):
        return ((y + dy + NY) % NY) * NZL + (zl + dz) % NZL

    here = block_at(0, 0)
    rows8 = amps[...].astype(F32)
    gath[0, core, here] = jnp.concatenate([rows8[:, :HALF], rows8[:, HALF:]], axis=0).astype(BF16)
    pl.semaphore_wait(barrier, len(partners))

    def hand_on(i, block):
        forwards.append(send(block, block, fwd_s.at[i], fwd_r.at[i], at(dc=1)))

    def step_x(i, index):
        for j in (1, 2):
            copy = send(
                gath.at[0, core, index], gath.at[j, core, index], x_s.at[j - 1, i], x_r.at[j - 1, i], at(dx=-X_OFF[j])
            )
            chunks[j].append(copy)

    mine = gath.at[0, core, here]
    blocks, forwards, chunks = [], [], [[] for _ in range(NX)]
    for i, (dy, dz) in enumerate(BLOCKS):
        blocks.append(send(mine, mine, blk_s.at[i], blk_r.at[i], at(dy=dy, dz=dz)))
    hand_on(len(BLOCKS), mine)
    step_x(len(BLOCKS), here)
    for i, (dy, dz) in enumerate(BLOCKS):
        blocks[i].wait_recv()
        there = block_at(-dy, -dz)
        step_x(i, there)
        hand_on(i, gath.at[0, core, there])

    def relay():
        part = slice(0, CHIPS // 2)
        chunks[3].append(send(gath.at[1, core, part], gath.at[3, core, part], x3_s.at[0], x3_r.at[0], at(dx=-1)))
        part = slice(CHIPS // 2, CHIPS)
        chunks[3].append(send(gath.at[2, core, part], gath.at[3, core, part], x3_s.at[1], x3_r.at[1], at(dx=1)))

    def merge(j, slot):
        for b in range(CHIPS):
            for h in range(2):
                lower = gath[j, 0, b].astype(F32)[8 * h:8 * h + 8]
                upper = gath[j, 1, b].astype(F32)[8 * h:8 * h + 8]
                rows = slice(slot * CHUNK + b * GROUP, slot * CHUNK + (b + 1) * GROUP)
                left[h, rows, :] = jnp.concatenate([lower, upper], axis=0).astype(BF16)

    def multiply(rows, chunks):
        dims = (((1,), (1,)), ((), ()))
        here = slice(0, chunks * CHUNK)
        product = lax.dot_general(left[0, here], ints[rows, :HALF], dims, preferred_element_type=F32)
        product += lax.dot_general(left[1, here], ints[rows, HALF:], dims, preferred_element_type=F32)
        rounded = product.astype(BF16)
        return [rounded[i * GROUP:(i + 1) * GROUP] for i in range(chunks * CHIPS)]

    def flip(blocks):
        n = blocks[0].shape[1] // WIDTH
        stack = jnp.concatenate([block[:, t * WIDTH:(t + 1) * WIDTH] for block in blocks for t in range(n)], axis=0)
        flipped = jnp.dot(stack, perm[...], preferred_element_type=F32)
        parts = [flipped[i * GROUP:(i + 1) * GROUP] for i in range(len(blocks) * n)]
        return [jnp.concatenate(parts[i * n:(i + 1) * n], axis=1) for i in range(len(blocks))]

    up, down, far = (occ + 1) % NOCC, (occ + 3) % NOCC, (occ + 2) % NOCC
    za = [[None] * 6 for _ in range(NX)]
    zb = [[None] * 6 for _ in range(NX)]
    ys = [[None] * 3 for _ in range(NX)]

    def out_rows(j, g):
        xx = (x + X_OFF[j] + NX) % NX
        return pl.ds(pl.multiple_of(g * 64 + xx * GROUP, GROUP), GROUP)

    def product_b(*js):
        found = multiply(slice(COLS_A, ROWS), len(js))
        for n, j in enumerate(js):
            for i in range(CHIPS):
                part_b[j, i % 2, i // 2] = found[n * CHIPS + i]
            ys[j][0] = send(part_b.at[j, 1 - half], mirr_b.at[j], y_s.at[j, 0], y_r.at[j, 0], at(dy=2))

    def first_b(j):
        ys[j][0].wait_recv()
        flipped = flip([mirr_b[j, k] for k in range(NOCC)])
        for k in range(NOCC):
            part_b[j, half, k] = (part_b[j, half, k].astype(F32) + flipped[k]).astype(BF16)
        plan = [
            (part_b.at[j, half, far, :, :MID], sum1_b.at[j, 0], 1),
            (part_b.at[j, half, far, :, MID:], sum1_b.at[j, 1], -1),
            (part_b.at[j, half, up, :, MID:], sum2_b.at[j, 0, 1], 1),
            (part_b.at[j, half, down, :, :MID], sum2_b.at[j, 1, 0], -1),
        ]
        for i, (src, dst, to) in enumerate(plan):
            zb[j][i] = send(src, dst, zb_s.at[j, i], zb_r.at[j, i], at(dh=to))

    def second_b(j):
        for i, who, columns, to in ((0, up, slice(0, MID), 1), (1, down, slice(MID, COLS_B), -1)):
            zb[j][i].wait_recv()
            total = part_b[j, half, who, :, columns].astype(F32) + sum1_b[j, i].astype(F32)
            part_b[j, half, who, :, columns] = total.astype(BF16)
            zb[j][4 + i] = send(
                part_b.at[j, half, who, :, columns], sum2_b.at[j, i, i], zb_s.at[j, 4 + i], zb_r.at[j, 4 + i], at(dh=to)
            )

    def total_b(j):
        for i in range(2, 6):
            zb[j][i].wait_recv()
        both = [jnp.concatenate([sum2_b[j, i, 0], sum2_b[j, i, 1]], axis=1).astype(F32) for i in range(2)]
        total = part_b[j, half, occ].astype(F32) + both[0] + both[1]
        back_b[j] = total.astype(BF16)
        ys[j][2] = send(back_b.at[j], done_b.at[j], y_s.at[j, 2], y_r.at[j, 2], at(dy=2))
        rows = out_rows(j, half)
        out[rows, COLS_A:] = total * inv[rows, COLS_A:]

    def finish_b(j):
        ys[j][2].wait_recv()
        rows = out_rows(j, 1 - half)
        out[rows, COLS_A:] = flip([done_b[j]])[0] * inv[rows, COLS_A:]

    def product_a(*js):
        found = multiply(slice(0, COLS_A), len(js))
        for n, j in enumerate(js):
            for i in range(CHIPS):
                part_a[j, i // 2, i % 2] = found[n * CHIPS + i]
            plan = [
                (part_a.at[j, far, 0], sum1_a.at[j, 0], 1),
                (part_a.at[j, far, 1], sum1_a.at[j, 1], -1),
                (part_a.at[j, up, 1], sum2_a.at[j, 0, 1], 1),
                (part_a.at[j, down, 0], sum2_a.at[j, 1, 0], -1),
            ]
            for i, (src, dst, to) in enumerate(plan):
                za[j][i] = send(src, dst, za_s.at[j, i], za_r.at[j, i], at(dh=to))

    def second_a(j):
        for i, who, to in ((0, up, 1), (1, down, -1)):
            za[j][i].wait_recv()
            part_a[j, who, i] = (part_a[j, who, i].astype(F32) + sum1_a[j, i].astype(F32)).astype(BF16)
            za[j][4 + i] = send(part_a.at[j, who, i], sum2_a.at[j, i, i], za_s.at[j, 4 + i], za_r.at[j, 4 + i], at(dh=to))

    def total_a(j):
        for i in range(2, 6):
            za[j][i].wait_recv()
        for g in range(2):
            total = part_a[j, occ, g].astype(F32) + sum2_a[j, 0, g].astype(F32) + sum2_a[j, 1, g].astype(F32)
            out[out_rows(j, g), :COLS_A] = total
            low_a[j, g] = total.astype(BF16)
        ys[j][1] = send(low_a.at[j], mirr_a.at[j], y_s.at[j, 1], y_r.at[j, 1], at(dy=2))

    def finish_a(j):
        ys[j][1].wait_recv()
        flipped = flip([mirr_a[j, g] for g in range(2)])
        for g in range(2):
            rows = out_rows(j, g)
            out[rows, :COLS_A] = (out[rows, :COLS_A] + flipped[g]) * inv[rows, :COLS_A]

    siblings = [None] * NX

    def pass_on(j):
        for copy in chunks[j]:
            copy.wait_recv()
        there = gath.at[j, core]
        siblings[j] = send(there, there, xf_s.at[j - 1], xf_r.at[j - 1], at(dc=1))

    def arrive(j, slot):
        siblings[j].wait_recv()
        merge(j, slot)

    def energies():
        for load in loads[1:5]:
            load.wait()
        sub = lax.broadcasted_iota(jnp.int32, (8, 128), 0)

        def pair_body(g, carry):
            rows = jnp.zeros((8, 128), F32)
            for i in range(8):
                pair = occ * SHARE + g * 8 + i
                energy = e_occ[pairs[0, pair]] + e_occ[pairs[1, pair]]
                rows = jnp.where(sub == i, energy, rows)
            pair_e[pl.ds(pl.multiple_of(g * 8, 8), 8), :] = rows
            return carry

        lax.fori_loop(0, SHARE // 8, pair_body, 0)
        lane = lax.broadcasted_iota(jnp.int32, (8, WIDTH), 1)
        lane_x, lane_y = lane // TILE, lane % TILE

        def tile_body(t, carry):
            first, second = tiles[0, t], tiles[1, t]
            a, b = jnp.maximum(first, 0) * TILE, jnp.maximum(second, 0) * TILE
            e_a = jnp.zeros((8, WIDTH), F32)
            e_b = jnp.zeros((8, WIDTH), F32)
            for i in range(TILE):
                e_a = jnp.where(lane_x == i, e_virt[a + i], e_a)
                e_b = jnp.where(lane_y == i, e_virt[b + i], e_b)
            energy = e_a + e_b
            keep = jnp.full((8, WIDTH), first, jnp.int32) >= 0
            columns = pl.ds(pl.multiple_of(t * WIDTH, WIDTH), WIDTH)
            for g in range(SHARE // 8):
                pair = pair_e[g * 8:(g + 1) * 8, :]
                denom = jnp.concatenate([pair, pair], axis=1) - energy
                inv[g * 8:(g + 1) * 8, columns] = jnp.where(keep, 1.0 / denom, 0.0)
            return carry

        lax.fori_loop(0, TILES, tile_body, 0)

    row_at = lax.broadcasted_iota(jnp.int32, (WIDTH, WIDTH), 0)
    col_at = lax.broadcasted_iota(jnp.int32, (WIDTH, WIDTH), 1)
    perm[...] = jnp.where(col_at == (row_at % TILE) * TILE + row_at // TILE, 1.0, 0.0).astype(BF16)
    for copy in forwards:
        copy.wait_recv()
    merge(0, 0)
    loads[5].wait()
    product_a(0)
    pass_on(1)
    product_b(0)
    pass_on(2)
    relay()
    arrive(1, 0)
    product_a(1)
    second_a(0)
    product_b(1)
    first_b(0)
    arrive(2, 0)
    product_a(2)
    second_a(1)
    product_b(2)
    pass_on(3)
    first_b(1)
    arrive(3, 0)
    product_a(3)
    second_a(2)
    product_b(3)
    energies()
    second_b(0)
    total_a(0)
    first_b(2)
    second_a(3)
    total_a(1)
    second_b(1)
    first_b(3)
    total_a(2)
    total_b(0)
    second_b(2)
    finish_a(0)
    total_a(3)
    total_b(1)
    second_b(3)
    finish_a(1)
    finish_b(0)
    total_b(2)
    finish_a(2)
    finish_b(1)
    finish_a(3)
    total_b(3)
    finish_b(2)
    finish_b(3)
    for copy in sends:
        copy.wait_send()


def per_device(integrals, amplitudes, tile_list, occ_pairs, e_occ, e_virt):
    dma = pltpu.SemaphoreType.DMA
    vmem, smem = pltpu.VMEM, pltpu.SMEM
    n_blocks = len(BLOCKS)
    operands = integrals, amplitudes, tile_list.T, occ_pairs.T, e_occ, e_virt
    operands = [pltpu.with_memory_space_constraint(operand, pltpu.HBM) for operand in operands]
    return pl.pallas_call(
        kernel,
        out_shape=jax.ShapeDtypeStruct((SHARE, ROWS), F32),
        in_specs=[pl.BlockSpec(memory_space=pltpu.HBM)] * 6,
        out_specs=pl.BlockSpec(memory_space=vmem),
        scratch_shapes=[
            vmem((ROWS, CD), BF16),
            vmem((8, CD), BF16),
            smem((2, TILES), jnp.int32),
            smem((2, PAIRS), jnp.int32),
            smem(e_occ.shape, F32),
            smem(e_virt.shape, F32),
            vmem((NX, NCORE, CHIPS, GROUP, HALF), BF16),
            vmem((2, 2 * CHUNK, HALF), BF16),
            vmem((NX, NOCC, 2, GROUP, COLS_A), BF16),
            vmem((NX, 2, GROUP, COLS_A), BF16),
            vmem((NX, 2, 2, GROUP, COLS_A), BF16),
            vmem((NX, 2, GROUP, COLS_A), BF16),
            vmem((NX, 2, GROUP, COLS_A), BF16),
            vmem((NX, 2, NOCC, GROUP, COLS_B), BF16),
            vmem((NX, NOCC, GROUP, COLS_B), BF16),
            vmem((NX, 2, GROUP, MID), BF16),
            vmem((NX, 2, 2, GROUP, MID), BF16),
            vmem((NX, GROUP, COLS_B), BF16),
            vmem((NX, GROUP, COLS_B), BF16),
            vmem((SHARE, ROWS), F32),
            vmem((SHARE, 128), F32),
            vmem((WIDTH, WIDTH), BF16),
            dma((6,)),
            dma((n_blocks,)), dma((n_blocks,)),
            dma((n_blocks + 1,)), dma((n_blocks + 1,)),
            dma((2, n_blocks + 1)), dma((2, n_blocks + 1)),
            dma((2,)), dma((2,)),
            dma((NX - 1,)), dma((NX - 1,)),
            dma((NX, 6)), dma((NX, 6)),
            dma((NX, 6)), dma((NX, 6)),
            dma((NX, 3)), dma((NX, 3)),
        ],
        compiler_params=pltpu.CompilerParams(
            collective_id=0, has_side_effects=True, vmem_limit_bytes=48 << 20
        ),
        cost_estimate=pl.CostEstimate(flops=2 * PAIRS * ROWS * CD, bytes_accessed=10 << 20, transcendentals=0),
    )(*operands)


def solution(mesh):
    placed = (P("loop", "occ"), P("loop", "occ"), P("loop", None), P(), P(), P())
    return jax.shard_map(
        per_device, mesh=mesh, in_specs=placed, out_specs=P("occ", "loop"), check_vma=False
    )
```
